1024 devices in a mesh: grp: 16 (over x, y), blk: 64 (over z, core).
Axes of the slice: x: 4, y: 4, z: 32, core: 2. Of those that a mesh axis runs over, the one named last changes fastest.
Arguments:
- charges: bfloat16 [64, 131072], P(None, ('grp', 'blk')), may hold values from -6 to 6
- near_blocks: bfloat16 [1024, 7, 128, 128], P(('grp', 'blk')), may hold values from -0.5 to 0.5
- near_offset: int32 [1024, 7], P(('grp', 'blk')), may hold values from -3 to 3, as said below
- near_count: int32 [1024], P(('grp', 'blk')), may hold values from 1 to 7, as said below
- far_group: int32 [1024, 48], P(('grp', 'blk')), may hold values from 0 to 15
- far_target: int32 [1024, 48, 1], P(('grp', 'blk')), may hold values from 0 to 63; in each aligned block of 48 rows (0 to 47, 48 to 95, ..., all dimensions but the last counted through in order) at most 2 rows name the same one
- far_v: bfloat16 [1024, 48, 32, 128], P(('grp', 'blk')), may hold values from -0.5 to 0.5
- far_u: bfloat16 [1024, 48, 32, 128], P(('grp', 'blk')), may hold values from -0.15625 to 0.15625
Outputs:
- potentials: bfloat16 [64, 131072], P(None, ('grp', 'blk'))
The draws below stay inside these ranges and needn't reach their ends.
Inputs may be any that keep to these rules, and one draw needn't show every extreme that they name: `near_offset`: the offsets of one device are distinct; the first near_count of them lead to a cluster of the same group. `near_count`: in every group some device has 7 live blocks. `far_target`: among the 48 blocks of one device no target is named more than 2 times; some device names one target exactly 2 times.
All inputs are finite; a program needn't handle non-finite values.
Results may differ from the reference program's by a relative error of at most 0.003.
Values may be sent and summed in bfloat16 or wider, within the bound.
No kernel may reach another device: no remote copies, remote signals or barrier semaphores. Data moves between devices by JAX's collectives and lax.ppermute only.
A program may use at most 32 MiB of HBM per device.

```python
import math
import jax
import jax.numpy as jnp
import numpy as np
from jax import lax

C = 128
RHS = 64
RANK = 32
FAR = 48
REACH = 3
NEAR = 7
CAP = 2
PANELS = 131072
N_GRP = 16
N_BLK = 64
DEVICES = 1024


def near_layout(key):
    devices = jnp.arange(DEVICES, dtype=jnp.int32)
    position = devices % N_BLK
    spread = jnp.arange(-REACH, REACH + 1, dtype=jnp.int32)
    reached = position[:, None] + spread[None, :]
    inside = (reached >= 0) & (reached < N_BLK)
    scores = jax.random.randint(jax.random.fold_in(key, 11), (DEVICES, NEAR), 0, 1 << 20) * NEAR + spread[None, :] + REACH
    sort_keys = jnp.where(inside, 0, 1 << 26) + scores
    ranking = jnp.argsort(sort_keys, axis=1, stable=True)
    offsets = jnp.take_along_axis(jnp.broadcast_to(spread, (DEVICES, NEAR)), ranking, axis=1)
    valid_count = jnp.sum(inside.astype(jnp.int32), axis=1)
    light_count = jax.random.randint(jax.random.fold_in(key, 12), (DEVICES,), 1, 5)
    heavy_pick = jax.random.randint(jax.random.fold_in(key, 13), (DEVICES,), 0, 8) == 0
    chosen = jax.random.randint(jax.random.fold_in(key, 14), (DEVICES // N_BLK,), REACH, N_BLK - REACH)
    forced = position == jnp.repeat(chosen, N_BLK)
    counts = jnp.minimum(jnp.where(heavy_pick | forced, NEAR, light_count), valid_count)
    return (offsets.astype(jnp.int32), counts.astype(jnp.int32))


def draw_near_offset(key, part):
    return near_layout(key)[0]


def draw_near_count(key, part):
    return near_layout(key)[1]


def touch_ends(array, rng, smallest, high):
    longest = array.shape.index(max(array.shape))
    spots = []
    for shift in (0, 1):
        where = [jax.random.randint(jax.random.fold_in(rng, axis), (), 0, length) for axis, length in enumerate(array.shape)]
        where[longest] = (where[longest] + shift) % array.shape[longest]
        spots.append(tuple(where))
    return array.at[spots[0]].set(smallest).at[spots[1]].set(high)


def steps_of(rng, extent, shards, low, largest):
    loudness = 1.0
    for dim, shards_of in shards:
        heights = jax.random.uniform(jax.random.fold_in(jax.random.fold_in(rng, 6), dim), (shards_of,), jnp.float32, low / len(shards), largest / len(shards))
        loudness = loudness * jnp.repeat(jnp.exp(heights), extent[dim] // shards_of).reshape((-1,) + (1,) * (len(extent) - 1 - dim))
    return loudness


def assign_block(rng, own, number, rows, count, top, most, skew):
    sequence = jax.random.permutation(rng, count)
    heavy_load, usual = shares(count, rows * top, most, skew, True), shares(count, rows * top, most, skew, False)
    places = jnp.arange(count)

    def named(sizes, offset_by):
        used = int((sizes > 0).sum())
        fixed = max(1, used // 4)
        moved = fixed + (places - fixed + offset_by * (used - fixed)) % max(1, count - fixed)
        return jnp.zeros((count,), jnp.int32).at[sequence[jnp.where(places < fixed, places, moved)]].set(jnp.asarray(sizes, jnp.int32))

    sizes = jnp.where(number % 4 == 0, named(heavy_load, number // 4), named(usual, number - number // 4 - 1))
    mixed = jax.random.permutation(jax.random.fold_in(own, 3), count)
    source_of, taker = mixed[0:count // 2 * 2:2], mixed[1:count // 2 * 2:2]
    margin = jnp.minimum(sizes[source_of] - 1, most - sizes[taker]) // 2
    margin = jnp.where((source_of == sequence[0]) | (taker == sequence[0]) | (sizes[taker] == 0), 0, jnp.maximum(margin, 0))
    moved = jax.random.randint(jax.random.fold_in(own, 4), (count // 2,), 0, 1 << 20) % (margin + 1)
    sizes = sizes.at[source_of].add(-moved).at[taker].add(moved)
    items = jnp.searchsorted(jnp.cumsum(sizes), jnp.arange(rows * top), side="right").astype(jnp.int32)
    table = items.reshape(top, rows).T
    table = table[jax.random.permutation(jax.random.fold_in(own, 1), rows)]
    offset_by = jax.random.randint(jax.random.fold_in(own, 2), (rows, 1), 0, top)
    return jnp.take_along_axis(table, (jnp.arange(top)[None, :] + offset_by) % top, axis=1)


def shares(amount, total, limit, slope, full):
    loads = [(1 << 20) // math.isqrt(grade ** slope) + 1 for grade in range(1, amount + 1)]
    largest = limit if full else min(limit, max(-(-total // amount), total * loads[0] // sum(loads)))
    least = 1 if total - largest >= amount - 1 else 0
    given, surplus = [largest] + [least] * (amount - 1), total - largest - least * (amount - 1)
    while surplus > 0:
        candidates = [i for i in range(1, amount) if given[i] < largest] or [i for i in range(1, amount) if given[i] < limit]
        pool, budget = sum([loads[i] for i in candidates]), surplus
        for i in candidates:
            more = min(limit - given[i], max(1, budget * loads[i] // pool), surplus)
            given[i] = given[i] + more
            surplus = surplus - more
    return np.array(given)


def normal_values(key, extent, scale, bound, cuts=(), kind=jnp.bfloat16):
    drawn = jax.random.normal(key, extent, jnp.float32) * scale
    if len(cuts) > 0:
        drawn = steps_of(key, extent, cuts, -0.22, 0.18) * drawn
    return jnp.clip(drawn, min=-bound, max=bound).astype(kind)


def setup_inputs(seed: int = 0) -> dict:
    arg_keys = jax.random.split(jax.random.key(seed), 9)
    charges = normal_values(arg_keys[0], (RHS, PANELS), 1.0, 6.0, ((1, 1024),))
    near_blocks = normal_values(arg_keys[1], (DEVICES, NEAR, C, C), C ** -0.5, 0.5, ((0, 1024),))
    near_offset = draw_near_offset(jax.random.fold_in(arg_keys[8], 71), 0)
    near_count = draw_near_count(jax.random.fold_in(arg_keys[8], 71), 0)
    far_group = touch_ends(jax.random.randint(arg_keys[4], (DEVICES, FAR), 0, N_GRP), jax.random.fold_in(arg_keys[4], 1), 0, N_GRP - 1).astype(jnp.int32)
    far_target_keys = jax.random.split(jax.random.fold_in(arg_keys[5], 1), DEVICES * FAR // FAR)
    far_target_turns = jax.random.permutation(jax.random.fold_in(arg_keys[5], 3), DEVICES * FAR // FAR)
    far_target = jax.vmap(lambda own, number: assign_block(jax.random.fold_in(arg_keys[5], 2), own, number, FAR, N_BLK, 1, CAP, 0))(far_target_keys, far_target_turns).reshape((DEVICES, FAR, 1))
    far_v = normal_values(arg_keys[6], (DEVICES, FAR, RANK, C), C ** -0.5, 0.5, ((0, 1024),))
    far_u = normal_values(arg_keys[7], (DEVICES, FAR, RANK, C), (RANK * FAR) ** -0.5, 0.15625, ((0, 1024),))
    return {"charges": charges, "near_blocks": near_blocks, "near_offset": near_offset, "near_count": near_count, "far_group": far_group, "far_target": far_target, "far_v": far_v, "far_u": far_u}


def reference(charges, near_blocks, near_offset, near_count, far_group, far_target, far_v, far_u):
    clusters = charges.reshape(RHS, N_GRP, N_BLK, C).transpose(1, 2, 0, 3)
    leaf_index = jnp.arange(N_BLK, dtype=jnp.int32)

    def one_group(pieces):
        own_charges, blocks, offsets, counts, groups_of, targets, factor_v, factor_u = pieces
        source_index = jnp.clip(leaf_index[:, None] + offsets, 0, N_BLK - 1)
        near_src = own_charges[source_index]
        active = jnp.arange(NEAR, dtype=jnp.int32)[None, :] < counts[:, None]
        near_src = jnp.where(active[:, :, None, None], near_src, jnp.zeros_like(near_src))
        near_sum = jnp.einsum('bkrs,bkts->brt', near_src.astype(jnp.float32), blocks.astype(jnp.float32))
        far_src = clusters[groups_of, leaf_index[:, None]]
        coefficients = jnp.einsum('bkrc,bkqc->bkrq', far_src.astype(jnp.float32), factor_v.astype(jnp.float32)).astype(jnp.bfloat16)
        partial_value = jnp.einsum('bkrq,bkqc->bkrc', coefficients.astype(jnp.float32), factor_u.astype(jnp.float32))
        selector = (targets[:, :, None] == leaf_index[None, None, :]).astype(jnp.float32)
        far_sum = jnp.einsum('bkt,bkrc->trc', selector, partial_value, precision=lax.Precision.HIGHEST)
        return (near_sum + far_sum).astype(jnp.bfloat16)

    grouped = (clusters,
               near_blocks.reshape(N_GRP, N_BLK, NEAR, C, C),
               near_offset.reshape(N_GRP, N_BLK, NEAR),
               near_count.reshape(N_GRP, N_BLK),
               far_group.reshape(N_GRP, N_BLK, FAR),
               far_target.reshape(N_GRP, N_BLK, FAR),
               far_v.reshape(N_GRP, N_BLK, FAR, RANK, C),
               far_u.reshape(N_GRP, N_BLK, FAR, RANK, C))
    result = lax.map(one_group, grouped)
    return result.transpose(2, 0, 1, 3).reshape(RHS, PANELS)
```

```python
import functools

import jax
import jax.numpy as jnp
from jax import lax
from jax.experimental import pallas as pl
from jax.experimental.pallas import tpu as pltpu
from jax.sharding import PartitionSpec as P

SEG = 4
VMEM = pltpu.VMEM
SMEM = pltpu.SMEM


def far_kernel(segs, group_ref, target_ref, place_ref, pooled_ref, v_ref, u_ref, out_ref):
    core, place = place_ref[0], place_ref[1]
    out_ref[...] = jnp.zeros_like(out_ref)
    blocks = v_ref.shape[0]
    step = 8
    for base in range(0, blocks, step):
        parts = []
        for k in range(base, base + step):
            coeff = lax.dot_general(
                pooled_ref[group_ref[0, k]],
                v_ref[k],
                (((1,), (1,)), ((), ())),
                preferred_element_type=jnp.float32,
            ).astype(jnp.bfloat16)
            parts.append(jnp.dot(coeff, u_ref[k], preferred_element_type=jnp.float32))
        for k, part in zip(range(base, base + step), parts):
            target = target_ref[0, k]
            chip = lax.shift_right_logical(target, 1)
            other = lax.bitwise_and(target + core, 1)
            ahead = lax.bitwise_and(chip - place, SEG - 1)
            slot = (other * SEG + ahead) * segs + lax.div(chip, SEG)
            out_ref[slot] += part


def far_parts(group, target, place, pooled, v, u, segs):
    blocks, rank, size = v.shape
    rhs = pooled.shape[1]
    return pl.pallas_call(
        functools.partial(far_kernel, segs),
        out_shape=jax.ShapeDtypeStruct((2 * SEG * segs, rhs, size), jnp.float32),
        in_specs=[pl.BlockSpec(memory_space=SMEM)] * 3 + [pl.BlockSpec(memory_space=VMEM)] * 3,
        out_specs=pl.BlockSpec(memory_space=VMEM),
        compiler_params=pltpu.CompilerParams(vmem_limit_bytes=24 << 20),
        cost_estimate=pl.CostEstimate(
            flops=4 * blocks * rhs * rank * size, bytes_accessed=4 << 20, transcendentals=0
        ),
        name="far_parts",
    )(group, target, place, pooled, v, u)


def near_kernel(offset_ref, count_ref, sources_ref, blocks_ref, out_ref):
    slots = blocks_ref.shape[0]
    total = jnp.zeros(out_ref.shape, jnp.float32)
    for k in range(slots):
        live = k < count_ref[0]
        source = sources_ref[offset_ref[0, k] + slots // 2]
        source = jnp.where(live, source, jnp.zeros_like(source))
        total += lax.dot_general(
            source, blocks_ref[k], (((1,), (1,)), ((), ())), preferred_element_type=jnp.float32
        )
    out_ref[...] = total


def near_sum(offset, count, sources, blocks):
    slots, size, _ = blocks.shape
    rhs = sources.shape[1]
    return pl.pallas_call(
        near_kernel,
        out_shape=jax.ShapeDtypeStruct((rhs, size), jnp.float32),
        in_specs=[pl.BlockSpec(memory_space=SMEM)] * 2 + [pl.BlockSpec(memory_space=VMEM)] * 2,
        out_specs=pl.BlockSpec(memory_space=VMEM),
        cost_estimate=pl.CostEstimate(
            flops=2 * slots * rhs * size * size, bytes_accessed=1 << 19, transcendentals=0
        ),
        name="near_sum",
    )(offset, count, sources, blocks)


def on_device(charges, near_blocks, near_offset, near_count, far_group, far_target, far_v, far_u):
    rhs, size = charges.shape
    groups, owners = lax.axis_size("grp"), lax.axis_size("blk")
    chips = owners // 2
    segs = chips // SEG
    me = lax.axis_index("blk")
    core, chip = me % 2, me // 2
    near_low = (near_blocks.shape[1] - 1) // 2

    pooled = lax.all_to_all(jnp.broadcast_to(charges[None], (groups, rhs, size)), "grp", 0, 0)

    place = jnp.stack([core, chip % SEG]).astype(jnp.int32)
    parts = far_parts(
        far_group, far_target[:, :, 0], place, pooled, far_v[0], far_u[0], segs
    ).reshape(2, SEG, segs, rhs, size)

    sibling = [(i, i ^ 1) for i in range(owners)]
    taken = lax.ppermute(
        jnp.concatenate([parts[1].reshape(-1, rhs, size), charges.astype(jnp.float32)[None]]),
        "blk",
        sibling,
    )
    other = taken[-1].astype(jnp.bfloat16)
    chip_sum = parts[0] + taken[:-1].reshape(SEG, segs, rhs, size)

    def turned(steps):
        pairs = []
        for i in range(owners):
            z, c = i // 2, i % 2
            pairs.append((i, ((z // SEG) * SEG + (z + steps) % SEG) * 2 + c))
        return pairs

    seg_sum = chip_sum[0]
    for steps in range(1, SEG):
        seg_sum = seg_sum + lax.ppermute(
            chip_sum[steps].astype(jnp.bfloat16), "blk", turned(steps)
        ).astype(jnp.float32)

    even = jnp.where(core == 0, charges, other)
    odd = jnp.where(core == 0, other, charges)
    pair = jnp.stack([even, odd])
    below = lax.ppermute(pair, "blk", [(i, i + 2) for i in range(owners - 2)])
    above = lax.ppermute(pair, "blk", [(i + 2, i) for i in range(owners - 2)])
    far_pairs = [(i, i + 3) for i in range(1, owners - 3, 2)] + [
        (i, i - 3) for i in range(4, owners, 2)
    ]
    third = lax.ppermute(charges, "blk", far_pairs)
    first = core == 0
    sources = jnp.stack(
        [
            jnp.where(first, third, below[0]),
            jnp.where(first, below[0], below[1]),
            jnp.where(first, below[1], other),
            charges,
            jnp.where(first, other, above[0]),
            jnp.where(first, above[0], above[1]),
            jnp.where(first, above[1], third),
        ]
    )
    near = near_sum(near_offset, near_count, sources, near_blocks[0])

    members = [
        [(s * SEG + z) * 2 + c for s in range(segs)] for z in range(SEG) for c in range(2)
    ]
    final = lax.all_to_all(
        seg_sum.astype(jnp.bfloat16), "blk", 0, 0, axis_index_groups=members
    )
    return (near + jnp.sum(final.astype(jnp.float32), axis=0)).astype(jnp.bfloat16)


def solution(mesh):
    placed = (
        P(None, ("grp", "blk")),
        P(("grp", "blk"), None, None, None),
        P(("grp", "blk"), None),
        P(("grp", "blk")),
        P(("grp", "blk"), None),
        P(("grp", "blk"), None, None),
        P(("grp", "blk"), None, None, None),
        P(("grp", "blk"), None, None, None),
    )
    return jax.shard_map(
        on_device, mesh=mesh, in_specs=placed, out_specs=P(None, ("grp", "blk")), check_vma=False
    )
```

```python
import functools

import jax
import jax.numpy as jnp
from jax import lax
from jax.experimental import pallas as pl
from jax.experimental.pallas import tpu as pltpu
from jax.sharding import PartitionSpec as P

VMEM = pltpu.VMEM
SMEM = pltpu.SMEM
REACH = 4


def local_call(kernel, outs, scalars, arrays, flops, name):
    return pl.pallas_call(
        kernel,
        out_shape=outs,
        in_specs=[pl.BlockSpec(memory_space=SMEM)]
        + [pl.BlockSpec(memory_space=VMEM)] * len(arrays),
        out_specs=jax.tree.map(lambda _: pl.BlockSpec(memory_space=VMEM), outs),
        compiler_params=pltpu.CompilerParams(vmem_limit_bytes=24 << 20),
        cost_estimate=pl.CostEstimate(
            flops=flops, bytes_accessed=sum(a.nbytes for a in arrays), transcendentals=0
        ),
        name=name,
    )(scalars, *arrays)


def times_transposed(a, b):
    return lax.dot_general(a, b, (((1,), (1,)), ((), ())), preferred_element_type=jnp.float32)


PLACES = 3


def far_kernel(chips, number_ref, pooled_ref, v_ref, u_ref, out_ref):
    blocks = v_ref.shape[0]
    here, core = number_ref[0], number_ref[1]
    half = chips // 2
    out_ref[: 2 * chips] = jnp.zeros((2 * chips, *out_ref.shape[1:]), jnp.float32)
    out_ref[2 * chips] = pooled_ref[number_ref[2]].astype(jnp.float32)
    step = 8
    for base in range(0, blocks, step):
        parts = []
        for k in range(base, base + step):
            coeff = times_transposed(pooled_ref[number_ref[PLACES + k]], v_ref[k])
            parts.append(
                jnp.dot(coeff.astype(jnp.bfloat16), u_ref[k], preferred_element_type=jnp.float32)
            )
        for k, part in zip(range(base, base + step), parts):
            target = number_ref[PLACES + blocks + k]
            ahead = lax.bitwise_and(lax.shift_right_logical(target, 1) - here, chips - 1)
            behind = (ahead >= half).astype(jnp.int32)
            steps = lax.bitwise_and(jnp.where(ahead >= half, chips - ahead, ahead), half - 1)
            slot = lax.bitwise_and(steps, REACH - 1) * (half // REACH)
            slot = slot + lax.div(steps, REACH)
            slot = slot * 2 + lax.bitwise_and(target, 1)
            slot = slot + lax.bitwise_xor(behind, core) * chips
            out_ref[slot] += part


def chip_kernel(number_ref, parts_ref, taken_ref, own_ref, mine_ref, over_ref, *sent_refs):
    size = own_ref.shape[0]
    core = number_ref[1]
    nearest = parts_ref[:2] + taken_ref[:2]
    own_ref[:2] = jnp.where(core == 0, nearest, jnp.zeros_like(nearest))
    over_ref[...] = nearest.astype(jnp.bfloat16)
    own_ref[2:] = parts_ref[2:size] + taken_ref[2:size]
    for step, sent_ref in enumerate(sent_refs, 1):
        at = pl.ds(step * size, size)
        sent_ref[:size] = (parts_ref[at] + taken_ref[at]).astype(jnp.bfloat16)
    mine = parts_ref[parts_ref.shape[0] - 1].astype(jnp.bfloat16)
    other = taken_ref[taken_ref.shape[0] - 1].astype(jnp.bfloat16)
    pair = jnp.stack([mine, other])
    mine_ref[...] = pair
    sent_refs[0][size:] = pair
    sent_refs[1][size] = other
    sent_refs[2][size : size + 2] = pair
    sent_refs[2][size + 2] = other


def gather_kernel(number_ref, opposite_ref, own_ref, *refs):
    del number_ref
    came_refs, keep_ref, sent_refs = refs[: REACH - 1], refs[REACH - 1], refs[REACH:]
    for hop in range(len(sent_refs) + 1):
        at = pl.ds(2 * hop, 2)
        total = own_ref[at]
        for came_ref in came_refs:
            total = total + came_ref[at].astype(jnp.float32)
        if hop == 0:
            keep_ref[...] = total
            continue
        if hop == len(sent_refs):
            total = total + opposite_ref[...].astype(jnp.float32)
        sent_refs[hop - 1][...] = total.astype(jnp.bfloat16)


def near_index(number_ref, first, slots, k):
    offset = number_ref[first + k]
    return jnp.where(number_ref[1] == 0, offset, -offset) + slots // 2


def near_kernel(first, number_ref, third_ref, next_ref, mine_ref, blocks_ref, out_ref):
    slots = blocks_ref.shape[0]
    count = number_ref[first + slots]
    last = next_ref.shape[0] - 1
    here = [third_ref[third_ref.shape[0] - 1], next_ref[last - 1], next_ref[last]]
    here += [mine_ref[0], mine_ref[1]]
    total = jnp.zeros(out_ref.shape, jnp.float32)
    for k in range(slots):
        place = near_index(number_ref, first, slots, k)
        live = k < count
        source = jnp.zeros_like(here[0])
        for i, cluster in enumerate(here):
            source = jnp.where(jnp.logical_and(live, place == i), cluster, source)
        total += times_transposed(source, blocks_ref[k])
    out_ref[...] = total


def hand_kernel(number_ref, next_ref, own_ref, *refs):
    came_refs, give_ref, keep_ref = refs[:-2], refs[-2], refs[-1]
    core = number_ref[1]
    total = own_ref[...]
    for came_ref in came_refs:
        total = total + came_ref[...].astype(jnp.float32)
    give_ref[0] = jnp.where(core == 0, total[1], total[0])
    keep_ref[...] = jnp.where(core == 0, total[0], total[1])
    give_ref[1:] = next_ref[next_ref.shape[0] - 2 :].astype(jnp.float32)


def final_kernel(first, number_ref, near_ref, keep_ref, came_ref, blocks_ref, out_ref):
    slots = blocks_ref.shape[0]
    count = number_ref[first + slots]
    total = near_ref[...] + keep_ref[...] + came_ref[0]
    for place, came in ((slots - 2, 2), (slots - 1, 1)):
        slot, found = jnp.int32(0), jnp.int32(0)
        for k in range(slots):
            hit = jnp.logical_and(k < count, near_index(number_ref, first, slots, k) == place)
            slot = jnp.where(hit, k, slot)
            found = jnp.where(hit, 1, found)
        source = came_ref[came]
        source = jnp.where(found == 1, source, jnp.zeros_like(source)).astype(jnp.bfloat16)
        total += times_transposed(source, blocks_ref[slot])
    out_ref[...] = total.astype(jnp.bfloat16)


def on_device(charges, near_blocks, near_offset, near_count, far_group, far_target, far_v, far_u):
    rhs, size = charges.shape
    groups, owners = lax.axis_size("grp"), lax.axis_size("blk")
    blocks, slots = far_v.shape[1], near_blocks.shape[1]
    rank = far_v.shape[2]
    chips = owners // 2
    hops = chips // 2 // REACH
    me = lax.axis_index("blk")
    place = jnp.stack(
        [lax.shift_right_logical(me, 1), lax.bitwise_and(me, 1), lax.axis_index("grp")]
    )
    numbers = jnp.concatenate(
        [place.astype(jnp.int32), far_group[0], far_target[0, :, 0], near_offset[0], near_count]
    )
    first = PLACES + 2 * blocks

    def f32(*shape):
        return jax.ShapeDtypeStruct((*shape, rhs, size), jnp.float32)

    def bf16(*shape):
        return jax.ShapeDtypeStruct((*shape, rhs, size), jnp.bfloat16)

    def around(value, steps):
        pairs = []
        for z in range(chips):
            pairs.append((2 * z, 2 * ((z + steps) % chips)))
            pairs.append((2 * z + 1, 2 * ((z - steps) % chips) + 1))
        return lax.ppermute(value, "blk", pairs)

    def across(value):
        return lax.ppermute(value, "blk", [(i, i ^ 1) for i in range(owners)])

    pooled = lax.all_to_all(jnp.broadcast_to(charges[None], (groups, rhs, size)), "grp", 0, 0)
    parts = local_call(
        functools.partial(far_kernel, chips),
        f32(2 * chips + 1),
        numbers,
        (pooled, far_v[0], far_u[0]),
        4 * blocks * rhs * rank * size,
        "far_parts",
    )

    taken = across(parts[chips:])
    own, mine, over, *sent = local_call(
        chip_kernel,
        [f32(2 * hops), bf16(2), bf16(2)] + [bf16(2 * hops + more) for more in (2, 1, 3)],
        numbers,
        (parts, taken),
        rhs * size,
        "chip_sums",
    )

    landed = {step: around(sent[step - 1], step) for step in (3, 2, 1)}
    opposite = lax.ppermute(
        over, "blk", [(2 * z + 1, 2 * ((z - REACH) % chips) + 1) for z in range(chips)]
    )
    keep, *sent = local_call(
        gather_kernel,
        [f32(2)] + [bf16(2)] * (hops - 1),
        numbers,
        (opposite, own, landed[3], landed[2], landed[1]),
        rhs * size,
        "first_step_sums",
    )

    came = [around(sent[hop - 1], hop * REACH) for hop in range(hops - 1, 0, -1)]

    near = local_call(
        functools.partial(near_kernel, first),
        f32(),
        numbers,
        (landed[2], landed[1], mine, near_blocks[0]),
        2 * slots * rhs * size * size,
        "near_sum",
    )

    give, keep = local_call(
        hand_kernel,
        [f32(3), f32()],
        numbers,
        (landed[1], keep, *came),
        rhs * size,
        "direction_sum",
    )
    return local_call(
        functools.partial(final_kernel, first),
        bf16(),
        numbers,
        (near, keep, across(give), near_blocks[0]),
        4 * rhs * size * size,
        "potentials",
    )


def solution(mesh):
    placed = (
        P(None, ("grp", "blk")),
        P(("grp", "blk"), None, None, None),
        P(("grp", "blk"), None),
        P(("grp", "blk")),
        P(("grp", "blk"), None),
        P(("grp", "blk"), None, None),
        P(("grp", "blk"), None, None, None),
        P(("grp", "blk"), None, None, None),
    )
    return jax.shard_map(
        on_device, mesh=mesh, in_specs=placed, out_specs=P(None, ("grp", "blk")), check_vma=False
    )
```

```python
import jax
import jax.numpy as jnp
from jax import lax
from jax.experimental import pallas as pl
from jax.experimental.pallas import tpu as pltpu
from jax.sharding import PartitionSpec as P

VMEM = pltpu.VMEM
SMEM = pltpu.SMEM
REACH = 4


def local_call(kernel, outs, scalars, arrays, flops, name):
    scalars = () if scalars is None else (scalars,)
    return pl.pallas_call(
        kernel,
        out_shape=outs,
        in_specs=[pl.BlockSpec(memory_space=SMEM)] * len(scalars)
        + [pl.BlockSpec(memory_space=VMEM)] * len(arrays),
        out_specs=jax.tree.map(lambda _: pl.BlockSpec(memory_space=VMEM), outs),
        compiler_params=pltpu.CompilerParams(vmem_limit_bytes=24 << 20),
        cost_estimate=pl.CostEstimate(
            flops=flops, bytes_accessed=sum(a.nbytes for a in arrays), transcendentals=0
        ),
        name=name,
    )(*scalars, *arrays)


def times_transposed(a, b):
    return lax.dot_general(a, b, (((1,), (1,)), ((), ())), preferred_element_type=jnp.float32)


def far_slots(target, here, core, chips):
    half = chips // 2
    ahead = lax.bitwise_and(lax.shift_right_logical(target, 1) - here, chips - 1)
    behind = (ahead >= half).astype(jnp.int32)
    steps = lax.bitwise_and(jnp.where(ahead >= half, chips - ahead, ahead), half - 1)
    slot = lax.bitwise_and(steps, REACH - 1) * (half // REACH) + lax.div(steps, REACH)
    slot = slot * 2 + lax.bitwise_and(target, 1)
    return slot + lax.bitwise_xor(behind, core) * chips


def far_kernel(number_ref, pooled_ref, v_ref, u_ref, out_ref, first_ref):
    blocks, last = v_ref.shape[0], out_ref.shape[0] - 1
    for slot in range(last):
        out_ref[slot] = jnp.zeros(out_ref.shape[1:], jnp.float32)
    first_ref[...] = jnp.where(
        number_ref[2 * blocks + 1] == 0,
        jnp.ones(first_ref.shape, jnp.float32),
        jnp.zeros(first_ref.shape, jnp.float32),
    )
    out_ref[last] = pooled_ref[number_ref[2 * blocks]].astype(jnp.float32)
    step = 16
    for base in range(0, blocks, step):
        parts = []
        for k in range(base, base + step):
            coeff = times_transposed(pooled_ref[number_ref[k]], v_ref[k])
            parts.append(
                jnp.dot(coeff.astype(jnp.bfloat16), u_ref[k], preferred_element_type=jnp.float32)
            )
        for k, part in zip(range(base, base + step), parts):
            out_ref[number_ref[blocks + k]] += part


def chip_kernel(first_ref, parts_ref, taken_ref, own_ref, mine_ref, over_ref, *sent_refs):
    size = own_ref.shape[0]
    nearest = parts_ref[:2] + taken_ref[:2]
    own_ref[:2] = jnp.where(first_ref[...] > 0, nearest, jnp.zeros_like(nearest))
    over_ref[...] = nearest.astype(jnp.bfloat16)
    own_ref[2:] = parts_ref[2:size] + taken_ref[2:size]
    for step, sent_ref in enumerate(sent_refs, 1):
        at = pl.ds(step * size, size)
        sent_ref[:size] = (parts_ref[at] + taken_ref[at]).astype(jnp.bfloat16)
    mine = parts_ref[parts_ref.shape[0] - 1].astype(jnp.bfloat16)
    other = taken_ref[taken_ref.shape[0] - 1].astype(jnp.bfloat16)
    pair = jnp.stack([mine, other])
    mine_ref[...] = pair
    sent_refs[0][size:] = pair
    sent_refs[1][size] = other
    sent_refs[2][size : size + 2] = pair
    sent_refs[2][size + 2] = other


def gather_kernel(*refs):
    (opposite_ref, *came_refs), own_ref, keep_ref = refs[:REACH], refs[REACH], refs[REACH + 1]
    sent_refs = refs[REACH + 2 :]
    for hop in range(len(sent_refs) + 1):
        at = pl.ds(2 * hop, 2)
        total = own_ref[at]
        for came_ref in came_refs:
            total = total + came_ref[at].astype(jnp.float32)
        if hop == 0:
            keep_ref[...] = total
            continue
        if hop == len(sent_refs):
            total = total + opposite_ref[...].astype(jnp.float32)
        sent_refs[hop - 1][...] = total.astype(jnp.bfloat16)


def near_kernel(
    number_ref, third_ref, next_ref, mine_ref, blocks_ref, out_ref, far_on_ref
):
    slots = blocks_ref.shape[0]
    last = next_ref.shape[0] - 1
    here = [third_ref[last - 1], next_ref[last - 1], next_ref[last], mine_ref[0], mine_ref[1]]
    total = jnp.zeros(out_ref.shape, jnp.float32)
    far_on = [(jnp.int32(0), jnp.int32(0))] * 2
    for k in range(slots):
        place = number_ref[k]
        source = jnp.zeros_like(here[0])
        for i, cluster in enumerate(here):
            source = jnp.where(place == i, cluster, source)
        total += times_transposed(source, blocks_ref[k])
        for i, (slot, found) in enumerate(far_on):
            hit = place == slots - 1 - i
            far_on[i] = (jnp.where(hit, k, slot), jnp.where(hit, 1, found))
    out_ref[...] = total
    for i, (slot, found) in enumerate(far_on):
        block = blocks_ref[slot]
        far_on_ref[i] = jnp.where(found == 1, block, jnp.zeros_like(block))


def hand_kernel(own_ref, *refs):
    came_refs, (next_ref, first_ref, give_ref, keep_ref) = refs[:-4], refs[-4:]
    core_0 = first_ref[...] > 0
    total = own_ref[...]
    for came_ref in came_refs:
        total = total + came_ref[...].astype(jnp.float32)
    give_ref[0] = jnp.where(core_0, total[1], total[0])
    keep_ref[...] = jnp.where(core_0, total[0], total[1])
    give_ref[1:] = next_ref[next_ref.shape[0] - 2 :].astype(jnp.float32)


def final_kernel(keep_ref, came_ref, near_ref, far_on_ref, out_ref):
    total = near_ref[...] + keep_ref[...] + came_ref[0]
    for i in range(2):
        total += times_transposed(came_ref[1 + i].astype(jnp.bfloat16), far_on_ref[i])
    out_ref[...] = total.astype(jnp.bfloat16)


def on_device(charges, near_blocks, near_offset, near_count, far_group, far_target, far_v, far_u):
    rhs, size = charges.shape
    groups, owners = lax.axis_size("grp"), lax.axis_size("blk")
    blocks, slots = far_v.shape[1], near_blocks.shape[1]
    rank = far_v.shape[2]
    chips = owners // 2
    hops = chips // 2 // REACH
    me = lax.axis_index("blk")
    here, core = lax.shift_right_logical(me, 1), lax.bitwise_and(me, 1)
    far_numbers = jnp.concatenate(
        [
            far_group[0],
            far_slots(far_target[0, :, 0], here, core, chips),
            lax.axis_index("grp")[None].astype(jnp.int32),
            core[None].astype(jnp.int32),
        ]
    )
    near_place = jnp.where(core == 0, near_offset[0], -near_offset[0]) + slots // 2
    near_place = jnp.where(jnp.arange(slots, dtype=jnp.int32) < near_count, near_place, slots)

    def f32(*shape):
        return jax.ShapeDtypeStruct((*shape, rhs, size), jnp.float32)

    def bf16(*shape):
        return jax.ShapeDtypeStruct((*shape, rhs, size), jnp.bfloat16)

    def around(value, steps):
        pairs = []
        for z in range(chips):
            pairs.append((2 * z, 2 * ((z + steps) % chips)))
            pairs.append((2 * z + 1, 2 * ((z - steps) % chips) + 1))
        return lax.ppermute(value, "blk", pairs)

    def across(value):
        return lax.ppermute(value, "blk", [(i, i ^ 1) for i in range(owners)])

    pooled = lax.all_to_all(jnp.broadcast_to(charges[None], (groups, rhs, size)), "grp", 0, 0)
    parts, is_first = local_call(
        far_kernel,
        [f32(2 * chips + 1), f32()],
        far_numbers,
        (pooled, far_v[0], far_u[0]),
        4 * blocks * rhs * rank * size,
        "far_parts",
    )

    taken = across(parts[chips:])
    own, mine, over, *sent = local_call(
        chip_kernel,
        [f32(2 * hops), bf16(2), bf16(2)] + [bf16(2 * hops + more) for more in (2, 1, 3)],
        None,
        (is_first, parts, taken),
        rhs * size,
        "chip_sums",
    )

    landed = {step: around(sent[step - 1], step) for step in (3, 2, 1)}
    opposite = lax.ppermute(
        over, "blk", [(2 * z + 1, 2 * ((z - REACH) % chips) + 1) for z in range(chips)]
    )
    keep, *sent = local_call(
        gather_kernel,
        [f32(2)] + [bf16(2)] * (hops - 1),
        None,
        (opposite, landed[3], landed[2], landed[1], own),
        rhs * size,
        "first_step_sums",
    )

    came = [around(sent[hop - 1], hop * REACH) for hop in range(hops - 1, 0, -1)]

    near, far_on = local_call(
        near_kernel,
        [f32(), jax.ShapeDtypeStruct((2, size, size), jnp.bfloat16)],
        near_place,
        (landed[2], landed[1], mine, near_blocks[0]),
        2 * slots * rhs * size * size,
        "near_sum",
    )

    give, keep = local_call(
        hand_kernel,
        [f32(3), f32()],
        None,
        (keep, *came, landed[1], is_first),
        rhs * size,
        "direction_sum",
    )
    return local_call(
        final_kernel,
        bf16(),
        None,
        (keep, across(give), near, far_on),
        4 * rhs * size * size,
        "potentials",
    )


def solution(mesh):
    placed = (
        P(None, ("grp", "blk")),
        P(("grp", "blk"), None, None, None),
        P(("grp", "blk"), None),
        P(("grp", "blk")),
        P(("grp", "blk"), None),
        P(("grp", "blk"), None, None),
        P(("grp", "blk"), None, None, None),
        P(("grp", "blk"), None, None, None),
    )
    return jax.shard_map(
        on_device, mesh=mesh, in_specs=placed, out_specs=P(None, ("grp", "blk")), check_vma=False
    )
```

```python
import jax
import jax.numpy as jnp
from jax import lax
from jax.experimental import pallas as pl
from jax.experimental.pallas import tpu as pltpu
from jax.sharding import PartitionSpec as P

VMEM = pltpu.VMEM
SMEM = pltpu.SMEM
REACH = 4


def local_call(kernel, outs, scalars, arrays, flops, name):
    scalars = () if scalars is None else (scalars,)
    return pl.pallas_call(
        kernel,
        out_shape=outs,
        in_specs=[pl.BlockSpec(memory_space=SMEM)] * len(scalars)
        + [pl.BlockSpec(memory_space=VMEM)] * len(arrays),
        out_specs=jax.tree.map(lambda _: pl.BlockSpec(memory_space=VMEM), outs),
        compiler_params=pltpu.CompilerParams(vmem_limit_bytes=24 << 20),
        cost_estimate=pl.CostEstimate(
            flops=flops, bytes_accessed=sum(a.nbytes for a in arrays), transcendentals=0
        ),
        name=name,
    )(*scalars, *arrays)


def times_transposed(a, b):
    return lax.dot_general(a, b, (((1,), (1,)), ((), ())), preferred_element_type=jnp.float32)


def far_slots(target, here, core, chips):
    half = chips // 2
    ahead = lax.bitwise_and(lax.shift_right_logical(target, 1) - here, chips - 1)
    behind = (ahead >= half).astype(jnp.int32)
    steps = lax.bitwise_and(jnp.where(ahead >= half, chips - ahead, ahead), half - 1)
    slot = lax.bitwise_and(steps, REACH - 1) * (half // REACH) + lax.div(steps, REACH)
    slot = slot * 2 + lax.bitwise_and(target, 1)
    return slot + lax.bitwise_xor(behind, core) * chips


def far_kernel(number_ref, pooled_ref, v_ref, u_ref, out_ref, first_ref):
    blocks, last = v_ref.shape[0], out_ref.shape[0] - 1
    for slot in range(last):
        out_ref[slot] = jnp.zeros(out_ref.shape[1:], jnp.float32)
    first_ref[...] = jnp.where(
        number_ref[2 * blocks + 1] == 0,
        jnp.ones(first_ref.shape, jnp.float32),
        jnp.zeros(first_ref.shape, jnp.float32),
    )
    out_ref[last] = pooled_ref[number_ref[2 * blocks]].astype(jnp.float32)
    step = 16
    for base in range(0, blocks, step):
        parts = []
        for k in range(base, base + step):
            coeff = times_transposed(pooled_ref[number_ref[k]], v_ref[k])
            parts.append(
                jnp.dot(coeff.astype(jnp.bfloat16), u_ref[k], preferred_element_type=jnp.float32)
            )
        for k, part in zip(range(base, base + step), parts):
            out_ref[number_ref[blocks + k]] += part


def chip_kernel(first_ref, parts_ref, taken_ref, own_ref, mine_ref, over_ref, *sent_refs):
    size = own_ref.shape[0]
    nearest = parts_ref[:2] + taken_ref[:2]
    own_ref[:2] = jnp.where(first_ref[...] > 0, nearest, jnp.zeros_like(nearest))
    over_ref[...] = nearest.astype(jnp.bfloat16)
    own_ref[2:] = parts_ref[2:size] + taken_ref[2:size]
    for step, sent_ref in enumerate(sent_refs, 1):
        at = pl.ds(step * size, size)
        sent_ref[:size] = (parts_ref[at] + taken_ref[at]).astype(jnp.bfloat16)
    mine = parts_ref[parts_ref.shape[0] - 1].astype(jnp.bfloat16)
    other = taken_ref[taken_ref.shape[0] - 1].astype(jnp.bfloat16)
    pair = jnp.stack([mine, other])
    mine_ref[...] = pair
    sent_refs[0][size:] = pair
    sent_refs[1][size] = other
    sent_refs[2][size : size + 2] = pair
    sent_refs[2][size + 2] = other


def gather_kernel(*refs):
    (opposite_ref, *came_refs), own_ref, keep_ref = refs[:REACH], refs[REACH], refs[REACH + 1]
    sent_refs = refs[REACH + 2 :]
    for hop in range(len(sent_refs) + 1):
        at = pl.ds(2 * hop, 2)
        total = own_ref[at]
        for came_ref in came_refs:
            total = total + came_ref[at].astype(jnp.float32)
        if hop == 0:
            keep_ref[...] = total
            continue
        if hop == len(sent_refs):
            total = total + opposite_ref[...].astype(jnp.float32)
        sent_refs[hop - 1][...] = total.astype(jnp.bfloat16)


def near_kernel(
    number_ref, third_ref, next_ref, mine_ref, blocks_ref, out_ref, far_on_ref
):
    slots = blocks_ref.shape[0]
    last = next_ref.shape[0] - 1
    here = [third_ref[last - 1], next_ref[last - 1], next_ref[last], mine_ref[0], mine_ref[1]]
    total = jnp.zeros(out_ref.shape, jnp.float32)
    far_on = [(jnp.int32(0), jnp.int32(0))] * 2
    for k in range(slots):
        place = number_ref[k]
        source = jnp.zeros_like(here[0])
        for i, cluster in enumerate(here):
            source = jnp.where(place == i, cluster, source)
        total += times_transposed(source, blocks_ref[k])
        for i, (slot, found) in enumerate(far_on):
            hit = place == slots - 1 - i
            far_on[i] = (jnp.where(hit, k, slot), jnp.where(hit, 1, found))
    out_ref[...] = total
    for i, (slot, found) in enumerate(far_on):
        block = blocks_ref[slot]
        far_on_ref[i] = jnp.where(found == 1, block, jnp.zeros_like(block))


def hand_kernel(own_ref, *refs):
    came_refs, (next_ref, first_ref, give_ref, keep_ref) = refs[:-4], refs[-4:]
    core_0 = first_ref[...] > 0
    total = own_ref[...]
    for came_ref in came_refs:
        total = total + came_ref[...].astype(jnp.float32)
    give_ref[0] = jnp.where(core_0, total[1], total[0])
    keep_ref[...] = jnp.where(core_0, total[0], total[1])
    give_ref[1:] = next_ref[next_ref.shape[0] - 2 :].astype(jnp.float32)


def final_kernel(keep_ref, came_ref, near_ref, far_on_ref, out_ref):
    total = near_ref[...] + keep_ref[...] + came_ref[0]
    for i in range(2):
        total += times_transposed(came_ref[1 + i].astype(jnp.bfloat16), far_on_ref[i])
    out_ref[...] = total.astype(jnp.bfloat16)


def on_device(charges, near_blocks, near_offset, near_count, far_group, far_target, far_v, far_u):
    rhs, size = charges.shape
    groups, owners = lax.axis_size("grp"), lax.axis_size("blk")
    blocks, slots = far_v.shape[1], near_blocks.shape[1]
    rank = far_v.shape[2]
    chips = owners // 2
    hops = chips // 2 // REACH
    me = lax.axis_index("blk")
    here, core = lax.shift_right_logical(me, 1), lax.bitwise_and(me, 1)
    far_numbers = jnp.concatenate(
        [
            groups - 1 - far_group[0],
            far_slots(far_target[0, :, 0], here, core, chips),
            (groups - 1 - lax.axis_index("grp"))[None].astype(jnp.int32),
            core[None].astype(jnp.int32),
        ]
    )
    near_place = jnp.where(core == 0, near_offset[0], -near_offset[0]) + slots // 2
    near_place = jnp.where(jnp.arange(slots, dtype=jnp.int32) < near_count, near_place, slots)

    def f32(*shape):
        return jax.ShapeDtypeStruct((*shape, rhs, size), jnp.float32)

    def bf16(*shape):
        return jax.ShapeDtypeStruct((*shape, rhs, size), jnp.bfloat16)

    def around(value, steps):
        pairs = []
        for z in range(chips):
            pairs.append((2 * z, 2 * ((z + steps) % chips)))
            pairs.append((2 * z + 1, 2 * ((z - steps) % chips) + 1))
        return lax.ppermute(value, "blk", pairs)

    def across(value):
        return lax.ppermute(value, "blk", [(i, i ^ 1) for i in range(owners)])

    pooled = lax.all_to_all(
        jnp.broadcast_to(charges[None], (groups, rhs, size)),
        "grp",
        0,
        0,
        axis_index_groups=[list(range(groups))[::-1]],
    )
    parts, is_first = local_call(
        far_kernel,
        [f32(2 * chips + 1), f32()],
        far_numbers,
        (pooled, far_v[0], far_u[0]),
        4 * blocks * rhs * rank * size,
        "far_parts",
    )

    taken = across(parts[chips:])
    own, mine, over, *sent = local_call(
        chip_kernel,
        [f32(2 * hops), bf16(2), bf16(2)] + [bf16(2 * hops + more) for more in (2, 1, 3)],
        None,
        (is_first, parts, taken),
        rhs * size,
        "chip_sums",
    )

    landed = {step: around(sent[step - 1], step) for step in (3, 2, 1)}
    opposite = lax.ppermute(
        over, "blk", [(2 * z + 1, 2 * ((z - REACH) % chips) + 1) for z in range(chips)]
    )
    keep, *sent = local_call(
        gather_kernel,
        [f32(2)] + [bf16(2)] * (hops - 1),
        None,
        (opposite, landed[3], landed[2], landed[1], own),
        rhs * size,
        "first_step_sums",
    )

    came = [around(sent[hop - 1], hop * REACH) for hop in range(hops - 1, 0, -1)]

    near, far_on = local_call(
        near_kernel,
        [f32(), jax.ShapeDtypeStruct((2, size, size), jnp.bfloat16)],
        near_place,
        (landed[2], landed[1], mine, near_blocks[0]),
        2 * slots * rhs * size * size,
        "near_sum",
    )

    give, keep = local_call(
        hand_kernel,
        [f32(3), f32()],
        None,
        (keep, *came, landed[1], is_first),
        rhs * size,
        "direction_sum",
    )
    return local_call(
        final_kernel,
        bf16(),
        None,
        (keep, across(give), near, far_on),
        4 * rhs * size * size,
        "potentials",
    )


def solution(mesh):
    placed = (
        P(None, ("grp", "blk")),
        P(("grp", "blk"), None, None, None),
        P(("grp", "blk"), None),
        P(("grp", "blk")),
        P(("grp", "blk"), None),
        P(("grp", "blk"), None, None),
        P(("grp", "blk"), None, None, None),
        P(("grp", "blk"), None, None, None),
    )
    return jax.shard_map(
        on_device, mesh=mesh, in_specs=placed, out_specs=P(None, ("grp", "blk")), check_vma=False
    )
```

```python
import jax
import jax.numpy as jnp
from jax import lax
from jax.experimental import pallas as pl
from jax.experimental.pallas import tpu as pltpu
from jax.sharding import PartitionSpec as P

VMEM = pltpu.VMEM
SMEM = pltpu.SMEM
REACH = 4


def local_call(kernel, outs, scalars, arrays, flops, name):
    scalars = () if scalars is None else (scalars,)
    return pl.pallas_call(
        kernel,
        out_shape=outs,
        in_specs=[pl.BlockSpec(memory_space=SMEM)] * len(scalars)
        + [pl.BlockSpec(memory_space=VMEM)] * len(arrays),
        out_specs=jax.tree.map(lambda _: pl.BlockSpec(memory_space=VMEM), outs),
        compiler_params=pltpu.CompilerParams(vmem_limit_bytes=24 << 20),
        cost_estimate=pl.CostEstimate(
            flops=flops, bytes_accessed=sum(a.nbytes for a in arrays), transcendentals=0
        ),
        name=name,
    )(*scalars, *arrays)


def times_transposed(a, b):
    return lax.dot_general(a, b, (((1,), (1,)), ((), ())), preferred_element_type=jnp.float32)


def far_slots(target, here, core, chips):
    half = chips // 2
    ahead = lax.bitwise_and(lax.shift_right_logical(target, 1) - here, chips - 1)
    behind = (ahead >= half).astype(jnp.int32)
    steps = lax.bitwise_and(jnp.where(ahead >= half, chips - ahead, ahead), half - 1)
    slot = lax.bitwise_and(steps, REACH - 1) * (half // REACH) + lax.div(steps, REACH)
    slot = slot * 2 + lax.bitwise_and(target, 1)
    return slot + lax.bitwise_xor(behind, core) * chips


def far_kernel(number_ref, pooled_ref, v_ref, u_ref, out_ref, first_ref):
    blocks, last = v_ref.shape[0], out_ref.shape[0] - 1
    for slot in range(last):
        out_ref[slot] = jnp.zeros(out_ref.shape[1:], jnp.float32)
    first_ref[...] = jnp.where(
        number_ref[2 * blocks + 1] == 0,
        jnp.ones(first_ref.shape, jnp.float32),
        jnp.zeros(first_ref.shape, jnp.float32),
    )
    out_ref[last] = pooled_ref[number_ref[2 * blocks]].astype(jnp.float32)
    step = 16
    for base in range(0, blocks, step):
        parts = []
        for k in range(base, base + step):
            coeff = times_transposed(pooled_ref[number_ref[k]], v_ref[k])
            parts.append(
                jnp.dot(coeff.astype(jnp.bfloat16), u_ref[k], preferred_element_type=jnp.float32)
            )
        for k, part in zip(range(base, base + step), parts):
            out_ref[number_ref[blocks + k]] += part


def chip_kernel(first_ref, parts_ref, taken_ref, own_ref, mine_ref, over_ref, *sent_refs):
    size = own_ref.shape[0]
    nearest = parts_ref[:2] + taken_ref[:2]
    own_ref[:2] = jnp.where(first_ref[...] > 0, nearest, jnp.zeros_like(nearest))
    over_ref[...] = nearest.astype(jnp.bfloat16)
    own_ref[2:] = parts_ref[2:size] + taken_ref[2:size]
    for step, sent_ref in enumerate(sent_refs, 1):
        at = pl.ds(step * size, size)
        sent_ref[:size] = (parts_ref[at] + taken_ref[at]).astype(jnp.bfloat16)
    mine = parts_ref[parts_ref.shape[0] - 1].astype(jnp.bfloat16)
    other = taken_ref[taken_ref.shape[0] - 1].astype(jnp.bfloat16)
    pair = jnp.stack([mine, other])
    mine_ref[...] = pair
    sent_refs[0][size:] = pair
    sent_refs[1][size] = other
    sent_refs[2][size:] = pair


def gather_kernel(*refs):
    (opposite_ref, *came_refs), own_ref, keep_ref = refs[:REACH], refs[REACH], refs[REACH + 1]
    sent_refs = refs[REACH + 2 :]
    for hop in range(len(sent_refs) + 1):
        at = pl.ds(2 * hop, 2)
        total = own_ref[at]
        for came_ref in came_refs:
            total = total + came_ref[at].astype(jnp.float32)
        if hop == 0:
            keep_ref[...] = total
            continue
        if hop == len(sent_refs):
            total = total + opposite_ref[...].astype(jnp.float32)
        sent_refs[hop - 1][...] = total.astype(jnp.bfloat16)


def near_kernel(
    number_ref, unused_ref, third_ref, next_ref, mine_ref, blocks_ref, out_ref, far_on_ref
):
    slots = blocks_ref.shape[0]
    last = next_ref.shape[0] - 1
    here = [third_ref[last - 1], next_ref[last - 1], next_ref[last], mine_ref[0], mine_ref[1]]
    total = jnp.zeros(out_ref.shape, jnp.float32)
    far_on = [(jnp.int32(0), jnp.int32(0))] * 2
    for k in range(slots):
        place = number_ref[k]
        source = jnp.zeros_like(here[0])
        for i, cluster in enumerate(here):
            source = jnp.where(place == i, cluster, source)
        total += times_transposed(source, blocks_ref[k])
        for i, (slot, found) in enumerate(far_on):
            hit = place == slots - 1 - i
            far_on[i] = (jnp.where(hit, k, slot), jnp.where(hit, 1, found))
    out_ref[...] = total
    for i, (slot, found) in enumerate(far_on):
        block = blocks_ref[slot]
        far_on_ref[i] = jnp.where(found == 1, block, jnp.zeros_like(block))


def hand_kernel(own_ref, *refs):
    came_refs, (next_ref, first_ref, give_ref, keep_ref) = refs[:-5], refs[-4:]
    core_0 = first_ref[...] > 0
    total = own_ref[...]
    for came_ref in came_refs:
        total = total + came_ref[...].astype(jnp.float32)
    give_ref[0] = jnp.where(core_0, total[1], total[0])
    keep_ref[...] = jnp.where(core_0, total[0], total[1])
    give_ref[1:] = next_ref[next_ref.shape[0] - 2 :].astype(jnp.float32)


def final_kernel(keep_ref, came_ref, near_ref, far_on_ref, out_ref):
    total = near_ref[...] + keep_ref[...] + came_ref[0]
    for i in range(2):
        total += times_transposed(came_ref[1 + i].astype(jnp.bfloat16), far_on_ref[i])
    out_ref[...] = total.astype(jnp.bfloat16)


def on_device(charges, near_blocks, near_offset, near_count, far_group, far_target, far_v, far_u):
    rhs, size = charges.shape
    groups, owners = lax.axis_size("grp"), lax.axis_size("blk")
    blocks, slots = far_v.shape[1], near_blocks.shape[1]
    rank = far_v.shape[2]
    chips = owners // 2
    lead = groups // 2 + groups // 8
    hops = chips // 2 // REACH
    me = lax.axis_index("blk")
    here, core = lax.shift_right_logical(me, 1), lax.bitwise_and(me, 1)
    far_numbers = jnp.concatenate(
        [
            lax.rem(lead + groups - far_group[0], groups),
            far_slots(far_target[0, :, 0], here, core, chips),
            lax.rem(lead + groups - lax.axis_index("grp"), groups)[None].astype(jnp.int32),
            core[None].astype(jnp.int32),
        ]
    )
    near_place = jnp.where(core == 0, near_offset[0], -near_offset[0]) + slots // 2
    near_place = jnp.where(jnp.arange(slots, dtype=jnp.int32) < near_count, near_place, slots)

    def f32(*shape):
        return jax.ShapeDtypeStruct((*shape, rhs, size), jnp.float32)

    def bf16(*shape):
        return jax.ShapeDtypeStruct((*shape, rhs, size), jnp.bfloat16)

    def around(value, steps):
        pairs = []
        for z in range(chips):
            pairs.append((2 * z, 2 * ((z + steps) % chips)))
            pairs.append((2 * z + 1, 2 * ((z - steps) % chips) + 1))
        return lax.ppermute(value, "blk", pairs)

    def across(value):
        return lax.ppermute(value, "blk", [(i, i ^ 1) for i in range(owners)])

    pooled = lax.all_to_all(
        jnp.broadcast_to(charges[None], (groups, rhs, size)),
        "grp",
        0,
        0,
        axis_index_groups=[[(lead - i) % groups for i in range(groups)]],
    )
    parts, is_first = local_call(
        far_kernel,
        [f32(2 * chips + 1), f32()],
        far_numbers,
        (pooled, far_v[0], far_u[0]),
        4 * blocks * rhs * rank * size,
        "far_parts",
    )

    taken = across(parts[chips:])
    own, mine, over, *sent = local_call(
        chip_kernel,
        [f32(2 * hops), bf16(2), bf16(2)] + [bf16(2 * hops + more) for more in (2, 1, 2)],
        None,
        (is_first, parts, taken),
        rhs * size,
        "chip_sums",
    )

    landed = {step: around(sent[step - 1], step) for step in (3, 2, 1)}
    opposite = lax.ppermute(
        over, "blk", [(2 * z + 1, 2 * ((z - REACH) % chips) + 1) for z in range(chips)]
    )
    keep, *sent = local_call(
        gather_kernel,
        [f32(2)] + [bf16(2)] * (hops - 1),
        None,
        (opposite, landed[3], landed[2], landed[1], own),
        rhs * size,
        "first_step_sums",
    )

    came = [around(sent[hop - 1], hop * REACH) for hop in range(hops - 1, 0, -1)]

    near, far_on = local_call(
        near_kernel,
        [f32(), jax.ShapeDtypeStruct((2, size, size), jnp.bfloat16)],
        near_place,
        (landed[3], landed[2], landed[1], mine, near_blocks[0]),
        2 * slots * rhs * size * size,
        "near_sum",
    )

    give, keep = local_call(
        hand_kernel,
        [f32(3), f32()],
        None,
        (keep, *came, landed[3], landed[1], is_first),
        rhs * size,
        "direction_sum",
    )
    return local_call(
        final_kernel,
        bf16(),
        None,
        (keep, across(give), near, far_on),
        4 * rhs * size * size,
        "potentials",
    )


def solution(mesh):
    placed = (
        P(None, ("grp", "blk")),
        P(("grp", "blk"), None, None, None),
        P(("grp", "blk"), None),
        P(("grp", "blk")),
        P(("grp", "blk"), None),
        P(("grp", "blk"), None, None),
        P(("grp", "blk"), None, None, None),
        P(("grp", "blk"), None, None, None),
    )
    return jax.shard_map(
        on_device, mesh=mesh, in_specs=placed, out_specs=P(None, ("grp", "blk")), check_vma=False
    )
```

```python
import jax
import jax.numpy as jnp
from jax import lax
from jax.experimental import pallas as pl
from jax.experimental.pallas import tpu as pltpu
from jax.sharding import PartitionSpec as P

VMEM = pltpu.VMEM
SMEM = pltpu.SMEM
REACH = 4


def local_call(kernel, outs, scalars, arrays, flops, name):
    scalars = () if scalars is None else (scalars,)
    return pl.pallas_call(
        kernel,
        out_shape=outs,
        in_specs=[pl.BlockSpec(memory_space=SMEM)] * len(scalars)
        + [pl.BlockSpec(memory_space=VMEM)] * len(arrays),
        out_specs=jax.tree.map(lambda _: pl.BlockSpec(memory_space=VMEM), outs),
        compiler_params=pltpu.CompilerParams(vmem_limit_bytes=24 << 20),
        cost_estimate=pl.CostEstimate(
            flops=flops, bytes_accessed=sum(a.nbytes for a in arrays), transcendentals=0
        ),
        name=name,
    )(*scalars, *arrays)


def times_transposed(a, b):
    return lax.dot_general(a, b, (((1,), (1,)), ((), ())), preferred_element_type=jnp.float32)


def far_slots(target, here, core, chips):
    half = chips // 2
    ahead = lax.bitwise_and(lax.shift_right_logical(target, 1) - here, chips - 1)
    behind = (ahead >= half).astype(jnp.int32)
    steps = lax.bitwise_and(jnp.where(ahead >= half, chips - ahead, ahead), half - 1)
    slot = lax.bitwise_and(steps, REACH - 1) * (half // REACH) + lax.div(steps, REACH)
    slot = slot * 2 + lax.bitwise_and(target, 1)
    return slot + lax.bitwise_xor(behind, core) * chips


def far_kernel(given_ref, pooled_ref, v_ref, u_ref, out_ref, first_ref, number_ref, done):
    blocks, last = v_ref.shape[0], out_ref.shape[0] - 1
    numbers = pltpu.make_async_copy(given_ref, number_ref, done)
    numbers.start()
    for slot in range(last):
        out_ref[slot] = jnp.zeros(out_ref.shape[1:], jnp.float32)
    numbers.wait()
    first_ref[...] = jnp.where(
        number_ref[2 * blocks + 1] == 0,
        jnp.ones(first_ref.shape, jnp.float32),
        jnp.zeros(first_ref.shape, jnp.float32),
    )
    out_ref[last] = pooled_ref[number_ref[2 * blocks]].astype(jnp.float32)
    step = 16
    for base in range(0, blocks, step):
        parts = []
        for k in range(base, base + step):
            coeff = times_transposed(pooled_ref[number_ref[k]], v_ref[k])
            parts.append(
                jnp.dot(coeff.astype(jnp.bfloat16), u_ref[k], preferred_element_type=jnp.float32)
            )
        for k, part in zip(range(base, base + step), parts):
            out_ref[number_ref[blocks + k]] += part


def chip_kernel(first_ref, parts_ref, taken_ref, own_ref, mine_ref, over_ref, *sent_refs):
    size = own_ref.shape[0]
    nearest = parts_ref[:2] + taken_ref[:2]
    own_ref[:2] = jnp.where(first_ref[...] > 0, nearest, jnp.zeros_like(nearest))
    over_ref[...] = nearest.astype(jnp.bfloat16)
    own_ref[2:] = parts_ref[2:size] + taken_ref[2:size]
    for step, sent_ref in enumerate(sent_refs, 1):
        at = pl.ds(step * size, size)
        sent_ref[:size] = (parts_ref[at] + taken_ref[at]).astype(jnp.bfloat16)
    mine = parts_ref[parts_ref.shape[0] - 1].astype(jnp.bfloat16)
    other = taken_ref[taken_ref.shape[0] - 1].astype(jnp.bfloat16)
    pair = jnp.stack([mine, other])
    mine_ref[...] = pair
    sent_refs[0][size:] = pair
    sent_refs[1][size] = other
    sent_refs[2][size:] = pair


def gather_kernel(*refs):
    (opposite_ref, *came_refs), own_ref, keep_ref = refs[:REACH], refs[REACH], refs[REACH + 1]
    sent_refs = refs[REACH + 2 :]
    for hop in range(len(sent_refs) + 1):
        at = pl.ds(2 * hop, 2)
        total = own_ref[at]
        for came_ref in came_refs:
            total = total + came_ref[at].astype(jnp.float32)
        if hop == 0:
            keep_ref[...] = total
            continue
        if hop == len(sent_refs):
            total = total + opposite_ref[...].astype(jnp.float32)
        sent_refs[hop - 1][...] = total.astype(jnp.bfloat16)


def near_kernel(
    number_ref, unused_ref, third_ref, next_ref, mine_ref, blocks_ref, out_ref, far_on_ref
):
    slots = blocks_ref.shape[0]
    last = next_ref.shape[0] - 1
    here = [third_ref[last - 1], next_ref[last - 1], next_ref[last], mine_ref[0], mine_ref[1]]
    total = jnp.zeros(out_ref.shape, jnp.float32)
    far_on = [(jnp.int32(0), jnp.int32(0))] * 2
    for k in range(slots):
        place = number_ref[k]
        source = jnp.zeros_like(here[0])
        for i, cluster in enumerate(here):
            source = jnp.where(place == i, cluster, source)
        total += times_transposed(source, blocks_ref[k])
        for i, (slot, found) in enumerate(far_on):
            hit = place == slots - 1 - i
            far_on[i] = (jnp.where(hit, k, slot), jnp.where(hit, 1, found))
    out_ref[...] = total
    for i, (slot, found) in enumerate(far_on):
        block = blocks_ref[slot]
        far_on_ref[i] = jnp.where(found == 1, block, jnp.zeros_like(block))


def hand_kernel(own_ref, *refs):
    came_refs, (next_ref, first_ref, give_ref, keep_ref) = refs[:-5], refs[-4:]
    core_0 = first_ref[...] > 0
    total = own_ref[...]
    for came_ref in came_refs:
        total = total + came_ref[...].astype(jnp.float32)
    give_ref[0] = jnp.where(core_0, total[1], total[0])
    keep_ref[...] = jnp.where(core_0, total[0], total[1])
    give_ref[1:] = next_ref[next_ref.shape[0] - 2 :].astype(jnp.float32)


def final_kernel(keep_ref, came_ref, near_ref, far_on_ref, out_ref):
    total = near_ref[...] + keep_ref[...] + came_ref[0]
    for i in range(2):
        total += times_transposed(came_ref[1 + i].astype(jnp.bfloat16), far_on_ref[i])
    out_ref[...] = total.astype(jnp.bfloat16)


def on_device(charges, near_blocks, near_offset, near_count, far_group, far_target, far_v, far_u):
    rhs, size = charges.shape
    groups, owners = lax.axis_size("grp"), lax.axis_size("blk")
    blocks, slots = far_v.shape[1], near_blocks.shape[1]
    rank = far_v.shape[2]
    chips = owners // 2
    lead = groups // 2 + groups // 8
    hops = chips // 2 // REACH
    me = lax.axis_index("blk")
    here, core = lax.shift_right_logical(me, 1), lax.bitwise_and(me, 1)
    far_numbers = jnp.concatenate(
        [
            lax.rem(lead + groups - far_group[0], groups),
            far_slots(far_target[0, :, 0], here, core, chips),
            lax.rem(lead + groups - lax.axis_index("grp"), groups)[None].astype(jnp.int32),
            core[None].astype(jnp.int32),
        ]
    )
    near_place = jnp.where(core == 0, near_offset[0], -near_offset[0]) + slots // 2
    near_place = jnp.where(jnp.arange(slots, dtype=jnp.int32) < near_count, near_place, slots)

    def f32(*shape):
        return jax.ShapeDtypeStruct((*shape, rhs, size), jnp.float32)

    def bf16(*shape):
        return jax.ShapeDtypeStruct((*shape, rhs, size), jnp.bfloat16)

    def around(value, steps):
        pairs = []
        for z in range(chips):
            pairs.append((2 * z, 2 * ((z + steps) % chips)))
            pairs.append((2 * z + 1, 2 * ((z - steps) % chips) + 1))
        return lax.ppermute(value, "blk", pairs)

    def across(value):
        return lax.ppermute(value, "blk", [(i, i ^ 1) for i in range(owners)])

    pooled = lax.all_to_all(
        jnp.broadcast_to(charges[None], (groups, rhs, size)),
        "grp",
        0,
        0,
        axis_index_groups=[[(lead - i) % groups for i in range(groups)]],
    )
    arrays = (far_numbers, pooled, far_v[0], far_u[0])
    parts, is_first = pl.pallas_call(
        far_kernel,
        out_shape=[f32(2 * chips + 1), f32()],
        in_specs=[pl.BlockSpec(memory_space=pl.ANY)] + [pl.BlockSpec(memory_space=VMEM)] * 3,
        out_specs=[pl.BlockSpec(memory_space=VMEM)] * 2,
        scratch_shapes=[
            pltpu.SMEM(far_numbers.shape, far_numbers.dtype),
            pltpu.SemaphoreType.DMA(()),
        ],
        compiler_params=pltpu.CompilerParams(vmem_limit_bytes=24 << 20),
        cost_estimate=pl.CostEstimate(
            flops=4 * blocks * rhs * rank * size,
            bytes_accessed=sum(a.nbytes for a in arrays),
            transcendentals=0,
        ),
        name="far_parts",
    )(*arrays)

    taken = across(parts[chips:])
    own, mine, over, *sent = local_call(
        chip_kernel,
        [f32(2 * hops), bf16(2), bf16(2)] + [bf16(2 * hops + more) for more in (2, 1, 2)],
        None,
        (is_first, parts, taken),
        rhs * size,
        "chip_sums",
    )

    landed = {step: around(sent[step - 1], step) for step in (3, 2, 1)}
    opposite = lax.ppermute(
        over, "blk", [(2 * z + 1, 2 * ((z - REACH) % chips) + 1) for z in range(chips)]
    )
    keep, *sent = local_call(
        gather_kernel,
        [f32(2)] + [bf16(2)] * (hops - 1),
        None,
        (opposite, landed[3], landed[2], landed[1], own),
        rhs * size,
        "first_step_sums",
    )

    came = [around(sent[hop - 1], hop * REACH) for hop in range(hops - 1, 0, -1)]

    near, far_on = local_call(
        near_kernel,
        [f32(), jax.ShapeDtypeStruct((2, size, size), jnp.bfloat16)],
        near_place,
        (landed[3], landed[2], landed[1], mine, near_blocks[0]),
        2 * slots * rhs * size * size,
        "near_sum",
    )

    give, keep = local_call(
        hand_kernel,
        [f32(3), f32()],
        None,
        (keep, *came, landed[3], landed[1], is_first),
        rhs * size,
        "direction_sum",
    )
    return local_call(
        final_kernel,
        bf16(),
        None,
        (keep, across(give), near, far_on),
        4 * rhs * size * size,
        "potentials",
    )


def solution(mesh):
    placed = (
        P(None, ("grp", "blk")),
        P(("grp", "blk"), None, None, None),
        P(("grp", "blk"), None),
        P(("grp", "blk")),
        P(("grp", "blk"), None),
        P(("grp", "blk"), None, None),
        P(("grp", "blk"), None, None, None),
        P(("grp", "blk"), None, None, None),
    )
    return jax.shard_map(
        on_device, mesh=mesh, in_specs=placed, out_specs=P(None, ("grp", "blk")), check_vma=False
    )
```
